32 devices in a mesh: dp: 8 (over z, x), mp: 4 (over y, core).
Axes of the slice: x: 2, y: 2, z: 4, core: 2. Of those that a mesh axis runs over, the one named last changes fastest.
Arguments:
- tokens: bfloat16 [4096, 1536], P(('dp', 'mp')), may hold values from -6 to 6
- cotangent: bfloat16 [4096, 1536], P(('dp', 'mp')), may hold values from -6 to 6
- doc_starts: int32 [8, 7], P('dp'), may hold values from 0 to 511, as said below
- valid_len: int32 [8], P('dp'), may hold values from 449 to 512
- gain_mixer: float32 [1536], replicated, may hold values from 0.5 to 1.5
- mixer_in_x: bfloat16 [1536, 3072], P(None, 'mp'), may hold values from -0.15625 to 0.15625
- mixer_in_z: bfloat16 [1536, 3072], P(None, 'mp'), may hold values from -0.15625 to 0.15625
- conv_weight: float32 [4, 3072], P(None, 'mp'), may hold values from -3 to 3
- conv_bias: float32 [3072], P('mp'), may hold values from -3 to 3
- mixer_proj: bfloat16 [3072, 128], P('mp'), may hold values from -0.109375 to 0.109375
- delta_proj: bfloat16 [96, 3072], P(None, 'mp'), may hold values from -0.625 to 0.625
- delta_bias: float32 [3072], P('mp'), may hold values from -4.6 to -1
- decay_log: float32 [3072, 16], P('mp'), may hold values from 0 to 2.77
- skip_weight: float32 [3072], P('mp'), may hold values from 0.5 to 1.5
- mixer_out: bfloat16 [3072, 1536], P('mp'), may hold values from -0.4375 to 0.4375
- gain_first: float32 [1536], replicated, may hold values from 0.5 to 1.5
- gate_first: bfloat16 [1536, 4096], P(None, 'mp'), may hold values from -0.15625 to 0.15625
- up_first: bfloat16 [1536, 4096], P(None, 'mp'), may hold values from -0.15625 to 0.15625
- down_first: bfloat16 [4096, 1536], P('mp'), may hold values from -0.09375 to 0.09375
- gain_attn: float32 [1536], replicated, may hold values from 0.5 to 1.5
- query_weight: bfloat16 [1536, 1536], P(None, 'mp'), may hold values from -0.15625 to 0.15625
- key_weight: bfloat16 [1536, 1536], P(None, 'mp'), may hold values from -0.15625 to 0.15625
- value_weight: bfloat16 [1536, 1536], P(None, 'mp'), may hold values from -0.15625 to 0.15625
- output_weight: bfloat16 [1536, 1536], P('mp'), may hold values from -0.625 to 0.625
- gain_second: float32 [1536], replicated, may hold values from 0.5 to 1.5
- gate_second: bfloat16 [1536, 4096], P(None, 'mp'), may hold values from -0.15625 to 0.15625
- up_second: bfloat16 [1536, 4096], P(None, 'mp'), may hold values from -0.15625 to 0.15625
- down_second: bfloat16 [4096, 1536], P('mp'), may hold values from -0.09375 to 0.09375
Outputs:
- mixed_out: bfloat16 [4096, 1536], P(('dp', 'mp'))
- input_grad: float32 [4096, 1536], P(('dp', 'mp'))
- grad_gain_mixer: float32 [1536], replicated
- grad_mixer_in_x: float32 [1536, 3072], P(None, 'mp')
- grad_mixer_in_z: float32 [1536, 3072], P(None, 'mp')
- grad_conv_weight: float32 [4, 3072], P(None, 'mp')
- grad_conv_bias: float32 [3072], P('mp')
- grad_mixer_proj: float32 [3072, 128], P('mp')
- grad_delta_proj: float32 [96, 3072], P(None, 'mp')
- grad_delta_bias: float32 [3072], P('mp')
- grad_decay_log: float32 [3072, 16], P('mp')
- grad_skip_weight: float32 [3072], P('mp')
- grad_mixer_out: float32 [3072, 1536], P('mp')
- grad_gain_first: float32 [1536], replicated
- grad_gate_first: float32 [1536, 4096], P(None, 'mp')
- grad_up_first: float32 [1536, 4096], P(None, 'mp')
- grad_down_first: float32 [4096, 1536], P('mp')
- grad_gain_attn: float32 [1536], replicated
- grad_query_weight: float32 [1536, 1536], P(None, 'mp')
- grad_key_weight: float32 [1536, 1536], P(None, 'mp')
- grad_value_weight: float32 [1536, 1536], P(None, 'mp')
- grad_output_weight: float32 [1536, 1536], P('mp')
- grad_gain_second: float32 [1536], replicated
- grad_gate_second: float32 [1536, 4096], P(None, 'mp')
- grad_up_second: float32 [1536, 4096], P(None, 'mp')
- grad_down_second: float32 [4096, 1536], P('mp')
The draws below stay inside these ranges and needn't reach their ends.
Inputs may be any that keep to these rules, and one draw needn't show every extreme that they name: `doc_starts`: in each row the entries rise strictly from a first entry of 0, and all lie below the row's valid_len; some row has a document starting at 511.
All inputs are finite; a program needn't handle non-finite values.
Results may differ from the reference program's by a relative error of at most 0.033.
Values may be sent and summed in bfloat16 or wider, within the bound.
No kernel may reach another device: no remote copies, remote signals or barrier semaphores. Data moves between devices by JAX's collectives and lax.ppermute only.
A program may use at most 448 MiB of HBM per device.

```python
import jax
import jax.numpy as jnp
from jax import lax

D = 1536
INNER = 3072
STATE = 16
CONV = 4
RANK = 96
FF = 4096
HEADS = 12
HDIM = 128
WINDOW = 2048
BLOCK_ROWS = 512
SCAN_BLOCK = 16
SEQ = 512
ROWS = 8
TOKENS = 4096


def document_layout(key):
    subkeys = jax.random.split(key, 8)
    row_number = jnp.arange(ROWS, dtype=jnp.int32)
    padding = jax.random.randint(subkeys[0], (ROWS,), 0, SEQ // 8)
    chosen = jax.random.randint(subkeys[1], (), 0, ROWS)
    padding = jnp.where(row_number == chosen, 0, jnp.where(row_number == (chosen + 1) % ROWS, SEQ // 8 - 1, padding))
    valid_length = (SEQ - padding).astype(jnp.int32)
    long_start = jax.random.randint(subkeys[2], (ROWS,), SEQ // 8, SEQ // 4)
    long_end = jax.random.randint(subkeys[3], (ROWS,), 3 * SEQ // 4 + 1, 13 * SEQ // 16)
    early_one = jax.random.randint(subkeys[4], (ROWS,), 1, long_start // 3 + 1)
    early_two = jax.random.randint(subkeys[5], (ROWS,), long_start // 3 + 1, 2 * long_start // 3 + 1)
    early_three = jax.random.randint(subkeys[6], (ROWS,), 2 * long_start // 3 + 1, long_start)
    late_one = jax.random.randint(subkeys[7], (ROWS,), long_end + 1, valid_length)
    late_one = jnp.where(row_number == chosen, SEQ - 1, late_one)
    starts = jnp.stack([jnp.zeros((ROWS,), jnp.int32), early_one, early_two, early_three, long_start, long_end, late_one], axis=1)
    return (starts.astype(jnp.int32), valid_length)


def draw_doc_starts(key, part):
    starts, valid_length = document_layout(key)
    return starts


def draw_valid_len(key, part):
    starts, valid_length = document_layout(key)
    return valid_length


def steps_of(stream_key, extent, shards, low, high):
    factor_of = 1.0
    for axis_at, shards_of in shards:
        draws = jax.random.uniform(jax.random.fold_in(jax.random.fold_in(stream_key, 6), axis_at), (shards_of,), jnp.float32, low / len(shards), high / len(shards))
        factor_of = factor_of * jnp.repeat(jnp.exp(draws), extent[axis_at] // shards_of).reshape((-1,) + (1,) * (len(extent) - 1 - axis_at))
    return factor_of


def centred(rng, shape, deviation, reach, shards=(), kind=jnp.bfloat16):
    values = jax.random.normal(rng, shape, jnp.float32) * deviation
    if len(shards) > 0:
        values = steps_of(rng, shape, shards, -0.22, 0.18) * values
    return jnp.clip(values, min=-reach, max=reach).astype(kind)


def setup_inputs(seed: int = 0) -> dict:
    arg_keys = jax.random.split(jax.random.key(seed), 29)
    return {
        "tokens": centred(arg_keys[0], (TOKENS, D), 1.0, 6.0, ((0, 32),)),
        "cotangent": centred(arg_keys[1], (TOKENS, D), 1.0, 6.0, ((0, 32),)),
        "doc_starts": draw_doc_starts(jax.random.fold_in(arg_keys[28], 71), 0),
        "valid_len": draw_valid_len(jax.random.fold_in(arg_keys[28], 71), 0),
        "gain_mixer": jnp.clip(1.0 + 0.1 * jax.random.normal(arg_keys[4], (D,), jnp.float32), 0.5, 1.5),
        "mixer_in_x": centred(arg_keys[5], (D, INNER), D ** -0.5, 0.15625, ((1, 4),)),
        "mixer_in_z": centred(arg_keys[6], (D, INNER), D ** -0.5, 0.15625, ((1, 4),)),
        "conv_weight": centred(arg_keys[7], (CONV, INNER), CONV ** -0.5, 3.0, ((1, 4),), jnp.float32),
        "conv_bias": centred(arg_keys[8], (INNER,), 0.5, 3.0, ((0, 4),), jnp.float32),
        "mixer_proj": centred(arg_keys[9], (INNER, RANK + 2 * STATE), INNER ** -0.5, 0.109375, ((0, 4),)),
        "delta_proj": centred(arg_keys[10], (RANK, INNER), RANK ** -0.5, 0.625, ((1, 4),)),
        "delta_bias": jnp.clip(-4.6 + 3.6 * jax.random.uniform(arg_keys[11], (INNER,), jnp.float32) ** steps_of(arg_keys[11], (INNER,), ((0, 4),), -0.2, 0.2), -4.6, -1.0),
        "decay_log": jnp.clip(2.77 * jax.random.uniform(arg_keys[12], (INNER, STATE), jnp.float32) ** steps_of(arg_keys[12], (INNER, STATE), ((0, 4),), -0.2, 0.2), 0.0, 2.77),
        "skip_weight": jnp.clip(0.5 + 1.0 * jax.random.uniform(arg_keys[13], (INNER,), jnp.float32) ** steps_of(arg_keys[13], (INNER,), ((0, 4),), -0.2, 0.2), 0.5, 1.5),
        "mixer_out": centred(arg_keys[14], (INNER, D), (INNER // 16) ** -0.5, 0.4375, ((0, 4),)),
        "gain_first": jnp.clip(1.0 + 0.1 * jax.random.normal(arg_keys[15], (D,), jnp.float32), 0.5, 1.5),
        "gate_first": centred(arg_keys[16], (D, FF), D ** -0.5, 0.15625, ((1, 4),)),
        "up_first": centred(arg_keys[17], (D, FF), D ** -0.5, 0.15625, ((1, 4),)),
        "down_first": centred(arg_keys[18], (FF, D), FF ** -0.5, 0.09375, ((0, 4),)),
        "gain_attn": jnp.clip(1.0 + 0.1 * jax.random.normal(arg_keys[19], (D,), jnp.float32), 0.5, 1.5),
        "query_weight": centred(arg_keys[20], (D, HEADS * HDIM), D ** -0.5, 0.15625, ((1, 4),)),
        "key_weight": centred(arg_keys[21], (D, HEADS * HDIM), D ** -0.5, 0.15625, ((1, 4),)),
        "value_weight": centred(arg_keys[22], (D, HEADS * HDIM), D ** -0.5, 0.15625, ((1, 4),)),
        "output_weight": centred(arg_keys[23], (HEADS * HDIM, D), (HEADS * HDIM // 16) ** -0.5, 0.625, ((0, 4),)),
        "gain_second": jnp.clip(1.0 + 0.1 * jax.random.normal(arg_keys[24], (D,), jnp.float32), 0.5, 1.5),
        "gate_second": centred(arg_keys[25], (D, FF), D ** -0.5, 0.15625, ((1, 4),)),
        "up_second": centred(arg_keys[26], (D, FF), D ** -0.5, 0.15625, ((1, 4),)),
        "down_second": centred(arg_keys[27], (FF, D), FF ** -0.5, 0.09375, ((0, 4),)),
    }


@jax.custom_vjp
def low(v):
    return lax.optimization_barrier(v.astype(jnp.bfloat16)).astype(jnp.float32)

@jax.custom_vjp
def low_back(v):
    return v

def low_keep(v):
    return (low(v), None)

def low_pass(kept, grad):
    return (grad,)

def back_keep(v):
    return (v, None)

def back_low(kept, grad):
    return (low(grad),)
low.defvjp(low_keep, low_pass)
low_back.defvjp(back_keep, back_low)
EPSILON = 1e-05
MASKED = -1e+30

def product(left_rows, weight):
    return jnp.dot(left_rows, weight, precision=lax.Precision.HIGHEST, preferred_element_type=jnp.float32)

def rms_apply(stream, gain_vec):
    return stream * lax.rsqrt(lax.optimization_barrier(jnp.mean(stream * stream, axis=-1, keepdims=True)) + EPSILON) * gain_vec

def document_ids(starts, length, seq_len):
    places = jnp.arange(seq_len, dtype=jnp.int32)
    counted = lax.optimization_barrier(jnp.sum((starts[None, :] <= places[:, None]).astype(jnp.int32), axis=1)) - 1
    return jnp.where(places < length, counted, starts.shape[0]).astype(jnp.int32)

def causal_conv(mixer_x, conv_weight, conv_bias, documents):
    running_sum = conv_bias[None, :] + conv_weight[0][None, :] * mixer_x
    for lag_steps in range(1, CONV):
        shifted = jnp.concatenate([jnp.zeros((lag_steps, mixer_x.shape[1]), mixer_x.dtype), mixer_x[:-lag_steps]], axis=0)
        before = jnp.concatenate([jnp.full((lag_steps,), -1, jnp.int32), documents[:-lag_steps]])
        same_doc = (before == documents).astype(mixer_x.dtype)
        running_sum = running_sum + conv_weight[lag_steps][None, :] * shifted * same_doc[:, None]
    return jax.nn.silu(running_sum)

def selective_scan(activated, delta_pre, input_map, output_map, decay_log, skip_weight, gating, carry_on):
    seq_len, channels = activated.shape
    delta_time = jax.nn.softplus(delta_pre)
    decay_rates = -jnp.exp(decay_log)
    block_count = seq_len // SCAN_BLOCK

    def one_block(hidden_state, pieces):
        act_block, delta_block, in_block, out_block, keep_block = pieces
        readouts = []
        for position in range(SCAN_BLOCK):
            factor = jnp.exp(delta_block[position][:, None] * decay_rates)
            hidden_state = keep_block[position] * factor * hidden_state + (delta_block[position] * act_block[position])[:, None] * in_block[position][None, :]
            readouts.append(lax.optimization_barrier(jnp.sum(hidden_state * out_block[position][None, :], axis=1)))
        return (hidden_state, jnp.stack(readouts))
    pieces = (activated.reshape(block_count, SCAN_BLOCK, channels), delta_time.reshape(block_count, SCAN_BLOCK, channels), input_map.reshape(block_count, SCAN_BLOCK, -1), output_map.reshape(block_count, SCAN_BLOCK, -1), carry_on.reshape(block_count, SCAN_BLOCK))
    initial = jnp.zeros((channels, decay_log.shape[1]), activated.dtype)
    _, readouts = lax.scan(jax.checkpoint(one_block), initial, pieces)
    result = readouts.reshape(seq_len, channels) + skip_weight[None, :] * activated
    return result * jax.nn.silu(gating)

def attention(queries, key_rows, value_rows, documents):
    seq_len = queries.shape[0]
    block_rows = min(BLOCK_ROWS, seq_len)
    block_count = seq_len // block_rows
    score_scale = HDIM ** (-0.5)
    places = jnp.arange(seq_len, dtype=jnp.int32)

    def one_block(pieces):
        query_block, start_row = pieces
        row_pos = start_row + jnp.arange(block_rows, dtype=jnp.int32)
        row_docs = lax.dynamic_slice_in_dim(documents, start_row, block_rows, 0)
        scores = jnp.einsum('qhd,khd->hqk', query_block, key_rows, precision=lax.Precision.HIGHEST) * score_scale
        scores = low_back(scores)
        allowed = (places[None, :] <= row_pos[:, None]) & (row_pos[:, None] - places[None, :] < WINDOW) & (documents[None, :] == row_docs[:, None])
        scores = jnp.where(allowed[None], scores, MASKED)
        row_max = lax.optimization_barrier(jnp.max(scores, axis=-1, keepdims=True))
        weights = jnp.exp(scores - row_max)
        attn_probs = weights / lax.optimization_barrier(jnp.sum(weights, axis=-1, keepdims=True))
        return jnp.einsum('hqk,khd->qhd', low(attn_probs), value_rows, precision=lax.Precision.HIGHEST)
    starts = (jnp.arange(block_count) * block_rows).astype(jnp.int32)
    blocks = queries.reshape(block_count, block_rows, queries.shape[1], queries.shape[2])
    result = lax.map(jax.checkpoint(one_block), (blocks, starts))
    return result.reshape(queries.shape)

def feed_forward(stream, gain_vec, gate_w, up_w, down_w):
    normed = low(rms_apply(stream, gain_vec))
    gate_act = low_back(product(normed, gate_w))
    up_act = low_back(product(normed, up_w))
    hidden = low(jax.nn.silu(gate_act) * up_act)
    return stream + low_back(product(hidden, down_w))

def row_forward(stream, params, documents, carry_on):
    gain_mixer, mixer_in_x, mixer_in_z, conv_weight, conv_bias, mixer_proj, delta_proj, delta_bias, decay_log, skip_weight, mixer_out, gain_first, gate_first, up_first, down_first, gain_attn, query_weight, key_weight, value_weight, output_weight, gain_second, gate_second, up_second, down_second = params
    seq_len = stream.shape[0]
    normed = low(rms_apply(stream, gain_mixer))
    mixer_x = low_back(product(normed, mixer_in_x))
    gate_values = low_back(product(normed, mixer_in_z))
    activated = causal_conv(mixer_x, conv_weight, conv_bias, documents)
    mixer_feats = low_back(product(low(activated), mixer_proj))
    delta_low = low(mixer_feats[:, :RANK])
    input_map = mixer_feats[:, RANK:RANK + STATE]
    output_map = mixer_feats[:, RANK + STATE:]
    delta_pre = low_back(product(delta_low, delta_proj) + delta_bias[None, :])
    scanned = selective_scan(activated, delta_pre, input_map, output_map, decay_log, skip_weight, gate_values, carry_on)
    stream_one = stream + low_back(product(low(scanned), mixer_out))
    stream_two = feed_forward(stream_one, gain_first, gate_first, up_first, down_first)
    normed_attn = low(rms_apply(stream_two, gain_attn))
    queries = low_back(low(product(normed_attn, query_weight))).reshape(seq_len, HEADS, HDIM)
    key_rows = low_back(low(product(normed_attn, key_weight))).reshape(seq_len, HEADS, HDIM)
    value_rows = low_back(low(product(normed_attn, value_weight))).reshape(seq_len, HEADS, HDIM)
    attended = attention(queries, key_rows, value_rows, documents)
    attended = low_back(low(attended.reshape(seq_len, HEADS * HDIM)))
    stream_three = stream_two + low_back(product(attended, output_weight))
    return feed_forward(stream_three, gain_second, gate_second, up_second, down_second)

def add_pair(left_sum, right_sum):
    return left_sum + right_sum

def reference(tokens, cotangent, doc_starts, valid_len, gain_mixer, mixer_in_x, mixer_in_z, conv_weight, conv_bias, mixer_proj, delta_proj, delta_bias, decay_log, skip_weight, mixer_out, gain_first, gate_first, up_first, down_first, gain_attn, query_weight, key_weight, value_weight, output_weight, gain_second, gate_second, up_second, down_second):
    params = tuple((weight.astype(jnp.float32) for weight in (gain_mixer, mixer_in_x, mixer_in_z, conv_weight, conv_bias, mixer_proj, delta_proj, delta_bias, decay_log, skip_weight, mixer_out, gain_first, gate_first, up_first, down_first, gain_attn, query_weight, key_weight, value_weight, output_weight, gain_second, gate_second, up_second, down_second)))
    streams = tokens.astype(jnp.float32).reshape(ROWS, SEQ, D)
    cot_rows = cotangent.astype(jnp.float32).reshape(ROWS, SEQ, D)

    def per_row(totals, pieces):
        stream, cot_row, starts, length = pieces
        documents = document_ids(starts, length, SEQ)
        before = jnp.concatenate([jnp.full((1,), -1, jnp.int32), documents[:-1]])
        carry_on = (before == documents).astype(jnp.float32)
        places = jnp.arange(SEQ, dtype=jnp.int32)
        live_rows = (places < length).astype(jnp.float32)

        def forward_only(stream_in, params_in):
            return row_forward(stream_in, params_in, documents, carry_on)
        result, backward = jax.vjp(forward_only, stream, params)
        d_input, dparams = backward(cot_row * live_rows[:, None])
        totals = jax.tree.map(add_pair, totals, dparams)
        return (totals, (result.astype(jnp.bfloat16), d_input))
    zero_grads = jax.tree.map(jnp.zeros_like, params)
    totals, (results, d_inputs) = lax.scan(per_row, zero_grads, (streams, cot_rows, doc_starts, valid_len))
    return (results.reshape(TOKENS, D), d_inputs.reshape(TOKENS, D), totals[0], totals[1], totals[2], totals[3], totals[4], totals[5], totals[6], totals[7], totals[8], totals[9], totals[10], totals[11], totals[12], totals[13], totals[14], totals[15], totals[16], totals[17], totals[18], totals[19], totals[20], totals[21], totals[22], totals[23])
```

```python
import math

import jax
import jax.numpy as jnp
from jax import lax
from jax.experimental import pallas as pl
from jax.experimental.pallas import tpu as pltpu
from jax.sharding import PartitionSpec as P

STATE = 16
CONV = 4
RANK = 96
HDIM = 128
WINDOW = 2048

EPSILON = 1e-05
MASKED = -1e30
LOG2E = math.log2(math.e)
STEP = 16
BLOCK = 64
LANES = 128
RESET = 1e30
f32 = jnp.float32
bf16 = jnp.bfloat16
MIB = 1024 * 1024


def product(left_rows, weight, kind=f32):
    return jnp.dot(left_rows, weight, preferred_element_type=f32).astype(kind)


def left_product(left_rows, right_rows, kind=f32):
    return lax.dot_general(
        left_rows, right_rows, (((0,), (0,)), ((), ())), preferred_element_type=f32
    ).astype(kind)


def right_product(left_rows, weight, kind=f32):
    return lax.dot_general(
        left_rows, weight, (((1,), (1,)), ((), ())), preferred_element_type=f32
    ).astype(kind)


def rms_apply(stream, gain_vec):
    return (
        stream * lax.rsqrt(jnp.mean(stream * stream, axis=-1, keepdims=True) + EPSILON) * gain_vec
    )


def document_ids(starts, length, seq_len):
    places = jnp.arange(seq_len, dtype=jnp.int32)
    counted = jnp.sum((starts[None, :] <= places[:, None]).astype(jnp.int32), axis=1) - 1
    return jnp.where(places < length, counted, starts.shape[0])


def causal_conv(mixer_x, conv_weight, conv_bias, documents):
    running_sum = conv_bias[None, :] + conv_weight[0][None, :] * mixer_x
    for lag_steps in range(1, CONV):
        shifted = jnp.concatenate(
            [jnp.zeros((lag_steps, mixer_x.shape[1]), mixer_x.dtype), mixer_x[:-lag_steps]], axis=0
        )
        before = jnp.concatenate([jnp.full((lag_steps,), -1, jnp.int32), documents[:-lag_steps]])
        same_doc = (before == documents).astype(mixer_x.dtype)
        running_sum = running_sum + conv_weight[lag_steps][None, :] * shifted * same_doc[:, None]
    return jax.nn.silu(running_sum)


def softplus(v):
    return jnp.maximum(v, 0.0) + jnp.log1p(jnp.exp(-jnp.abs(v)))

def lane_fold(v):
    total = v[:, :128]
    for j in range(1, v.shape[1] // 128):
        total = total + v[:, 128 * j:128 * (j + 1)]
    return total

def scan_fwd_kernel(act_ref, pre_ref, gate_ref, keep_ref, b_ref, c_ref, rate_ref, skip_ref,
                    out_ref, res_ref, hs_ref, h_ref, dk_ref, u_ref):
    @pl.when(pl.program_id(0) == 0)
    def _():
        h_ref[...] = jnp.zeros_like(h_ref)
    tb = act_ref.shape[0]
    delta = softplus(pre_ref[...])
    dk_ref[...] = jnp.where(keep_ref[...][:, :1] > 0.0, delta, RESET)
    u_ref[...] = delta * act_ref[...]
    rate2 = rate_ref[...] * LOG2E
    lanes = act_ref.shape[1]

    def body(k, h):
        base = pl.multiple_of(k * STEP, STEP)
        rows = []
        for i in range(STEP):
            dk = dk_ref[pl.ds(base + i, 1), :]
            u = u_ref[pl.ds(base + i, 1), :]
            bt = jnp.concatenate([b_ref[base + i]] * (lanes // 128), axis=1)
            ct = jnp.concatenate([c_ref[base + i]] * (lanes // 128), axis=1)
            h = jnp.exp2(dk * rate2) * h + u * bt
            hs_ref[base + i] = h.astype(hs_ref.dtype)
            rows.append(jnp.sum(h * ct, axis=0, keepdims=True))
        read = jnp.concatenate(rows, axis=0)
        res = read + skip_ref[...] * act_ref[pl.ds(base, STEP), :]
        res_ref[pl.ds(base, STEP), :] = res
        g = gate_ref[pl.ds(base, STEP), :]
        out_ref[pl.ds(base, STEP), :] = (res * g * jax.nn.sigmoid(g)).astype(out_ref.dtype)
        return h

    h_ref[...] = lax.fori_loop(0, tb // STEP, body, h_ref[...])


def scan_fwd(act, pre, gate, keep_b, b_b, c_b, rate_t, skip, tb=BLOCK, hs_dtype=f32):
    t, c = act.shape
    n = rate_t.shape[0]
    tb = min(tb, t)
    row = pl.BlockSpec((tb, c), lambda i: (i, 0))
    return pl.pallas_call(
        scan_fwd_kernel,
        grid=(t // tb,),
        in_specs=[row, row, row, pl.BlockSpec((tb, 128), lambda i: (i, 0)),
                  pl.BlockSpec((tb, n, 128), lambda i: (i, 0, 0)),
                  pl.BlockSpec((tb, n, 128), lambda i: (i, 0, 0)),
                  pl.BlockSpec((n, c), lambda i: (0, 0)),
                  pl.BlockSpec((1, c), lambda i: (0, 0))],
        out_specs=[row, row, pl.BlockSpec((tb, n, c), lambda i: (i, 0, 0))],
        out_shape=[jax.ShapeDtypeStruct((t, c), bf16),
                   jax.ShapeDtypeStruct((t, c), f32),
                   jax.ShapeDtypeStruct((t, n, c), hs_dtype)],
        scratch_shapes=[pltpu.VMEM((n, c), f32), pltpu.VMEM((tb, c), f32),
                        pltpu.VMEM((tb, c), f32)],
        compiler_params=pltpu.CompilerParams(vmem_limit_bytes=20 * MIB),
        cost_estimate=pl.CostEstimate(flops=t * c * n * 40, bytes_accessed=t * c * 100, transcendentals=t * c * n),
        name="scan_forward",
    )(act, pre, gate, keep_b, b_b, c_b, rate_t, skip)


def scan_bwd_kernel(carried, act_ref, pre_ref, gate_ref, res_ref, ds_ref, keep_ref, b_ref, c_ref,
                    rate_ref, skip_ref, hs_ref, hp_ref, *refs):
    if carried:
        before, refs = refs[:9], refs[9:]
    (dact_ref, dpre_ref, dgate_ref, db_ref, dc_ref, drate_ref, dskip_ref, dbias_ref, g_ref,
     dk_ref, u_ref, dl_ref, dy_ref, wide_b_ref, wide_c_ref) = refs

    @pl.when(pl.program_id(0) == 0)
    def _():
        for n, ref in ((5, drate_ref), (6, dskip_ref), (7, dbias_ref), (8, g_ref)):
            ref[...] = before[n][...] if carried else jnp.zeros_like(ref)

    tb = act_ref.shape[0]
    lanes = act_ref.shape[1]
    delta = softplus(pre_ref[...])
    dl_ref[...] = delta
    dk_ref[...] = jnp.where(keep_ref[...][:, :1] > 0.0, delta, RESET)
    u_ref[...] = delta * act_ref[...]
    gate = gate_ref[...]
    sg = jax.nn.sigmoid(gate)
    ds = ds_ref[...]
    dgate_ref[...] = (ds * res_ref[...] * sg * (1.0 + gate * (1.0 - sg))).astype(dgate_ref.dtype)
    dy = ds * gate * sg
    dy_ref[...] = dy
    dskip_ref[...] += jnp.sum(dy * act_ref[...], axis=0, keepdims=True)
    rate = rate_ref[...]
    rate2 = rate * LOG2E
    nk = tb // STEP

    def body(kk, carry):
        g, drate = carry
        k = nk - 1 - kk
        base = pl.multiple_of(k * STEP, STEP)
        r1s = [None] * STEP
        r2s = [None] * STEP
        h = hs_ref[base + STEP - 1]
        for i in range(STEP - 1, -1, -1):
            dk = dk_ref[pl.ds(base + i, 1), :]
            u = u_ref[pl.ds(base + i, 1), :]
            dyr = dy_ref[pl.ds(base + i, 1), :]
            dl = dl_ref[pl.ds(base + i, 1), :]
            bt = jnp.concatenate([b_ref[base + i]] * (lanes // 128), axis=1)
            ct = jnp.concatenate([c_ref[base + i]] * (lanes // 128), axis=1)
            wide_c_ref[base + i] = lane_fold(h * dyr)
            if i > 0:
                hprev = hs_ref[base + i - 1]
            else:
                inside = hs_ref[jnp.maximum(base - 1, 0)]
                hprev = jnp.where(base > 0, inside, hp_ref[hp_ref.shape[0] - 1])
            lam = g + ct * dyr
            wide_b_ref[base + i] = lane_fold(lam * u)
            r2s[i] = jnp.sum(lam * bt, axis=0, keepdims=True)
            g = jnp.exp2(dk * rate2) * lam
            w = g * hprev
            drate = drate + w * dl
            r1s[i] = jnp.sum(w * rate, axis=0, keepdims=True)
            h = hprev
        r1 = jnp.concatenate(r1s, axis=0)
        r2 = jnp.concatenate(r2s, axis=0)
        sl = pl.ds(base, STEP)
        a = act_ref[sl, :]
        d_delta = r1 + a * r2
        dpre = (d_delta * jax.nn.sigmoid(pre_ref[sl, :])).astype(bf16)
        dpre_ref[sl, :] = dpre
        dact_ref[sl, :] = dl_ref[sl, :] * r2 + skip_ref[...] * dy_ref[sl, :]
        dbias_ref[...] += jnp.sum(dpre.astype(f32), axis=0, keepdims=True)
        return (g, drate)

    g, drate = lax.fori_loop(0, nk, body, (g_ref[...], jnp.zeros_like(g_ref)))
    g_ref[...] = g
    drate_ref[...] += drate
    db_ref[...] = jnp.sum(wide_b_ref[...], axis=2)
    dc_ref[...] = jnp.sum(wide_c_ref[...], axis=2)


def scan_bwd(act, pre, gate, res, ds, keep_b, b_b, c_b, rate_t, skip, hs, before=None, tb=BLOCK):
    t, c = act.shape
    n = rate_t.shape[0]
    nb = t // tb
    steps = nb // 2
    top = nb - 1 if before is None else steps - 1
    row = pl.BlockSpec((tb, c), lambda i: (top - i, 0))
    one = pl.BlockSpec((1, c), lambda i: (0, 0))
    state = pl.BlockSpec((n, c), lambda i: (0, 0))
    bl = pl.BlockSpec((tb, n, 128), lambda i: (top - i, 0, 0))
    maps = pl.BlockSpec((tb, n), lambda i: (top - i, 0))
    per = tb // 8
    shapes = [
        ((t, c), f32), ((t, c), bf16), ((t, c), bf16), ((t, n), f32), ((t, n), f32),
        ((n, c), f32), ((1, c), f32), ((1, c), f32), ((n, c), f32),
    ]
    held = pl.BlockSpec(memory_space=pltpu.HBM)
    carried = before is not None
    return pl.pallas_call(
        lambda *refs: scan_bwd_kernel(carried, *refs),
        grid=(steps,),
        in_specs=[row, row, row, row, row, pl.BlockSpec((tb, 128), lambda i: (top - i, 0)),
                  bl, bl, state, one,
                  pl.BlockSpec((tb, n, c), lambda i: (top - i, 0, 0)),
                  pl.BlockSpec((8, n, c), lambda i: (jnp.maximum((top - i) * per - 1, 0), 0, 0))]
        + ([held] * 5 + [state, one, one, state] if carried else []),
        out_specs=[row, row, row, maps, maps, state, one, one, state],
        out_shape=[jax.ShapeDtypeStruct(*shape) for shape in shapes],
        input_output_aliases={12 + k: k for k in range(5)} if carried else {},
        scratch_shapes=[pltpu.VMEM((tb, c), f32)] * 4 + [pltpu.VMEM((tb, n, 128), f32)] * 2,
        compiler_params=pltpu.CompilerParams(vmem_limit_bytes=28 * MIB),
        cost_estimate=pl.CostEstimate(flops=t * c * n * 100, bytes_accessed=t * c * 100, transcendentals=t * c * n),
        name="scan_backward",
    )(act, pre, gate, res, ds, keep_b, b_b, c_b, rate_t, skip, hs, hs, *(before or ()))


def visible(docs_row_ref, docs_col_ref):
    seq_len = docs_row_ref.shape[1]
    row_pos = lax.broadcasted_iota(jnp.int32, (seq_len, seq_len), 0)
    places = lax.broadcasted_iota(jnp.int32, (seq_len, seq_len), 1)
    same = docs_row_ref[0:1, :] == docs_col_ref[:, 0:1]
    return (places <= row_pos) & (row_pos - places < WINDOW) & same


def probabilities(queries, key_rows, allowed):
    scores = right_product(queries, key_rows) * HDIM ** (-0.5)
    scores = jnp.where(allowed, scores, MASKED)
    weights = jnp.exp(scores - jnp.max(scores, axis=-1, keepdims=True))
    return weights / jnp.sum(weights, axis=-1, keepdims=True)


def attend_forward_kernel(q_ref, k_ref, v_ref, docs_row_ref, docs_col_ref, out_ref):
    allowed = visible(docs_row_ref, docs_col_ref)
    for start in range(0, q_ref.shape[1], HDIM):
        head = slice(start, start + HDIM)
        probs = probabilities(q_ref[:, head], k_ref[:, head], allowed).astype(bf16)
        out_ref[:, head] = product(probs, v_ref[:, head], bf16)


def attend_backward_kernel(q_ref, k_ref, v_ref, d_ref, docs_row_ref, docs_col_ref, out_ref):
    allowed = visible(docs_row_ref, docs_col_ref)
    width = q_ref.shape[1]
    score_scale = HDIM ** (-0.5)
    for start in range(0, width, HDIM):
        head = slice(start, start + HDIM)
        queries, key_rows, d_out = q_ref[:, head], k_ref[:, head], d_ref[:, head]
        probs = probabilities(queries, key_rows, allowed)
        d_probs = right_product(d_out, v_ref[:, head])
        inner = jnp.sum(probs * d_probs, axis=-1, keepdims=True)
        d_scores = (probs * (d_probs - inner)).astype(bf16)
        out_ref[:, head] = (product(d_scores, key_rows) * score_scale).astype(bf16)
        out_ref[:, width + start : width + start + HDIM] = (
            left_product(d_scores, queries) * score_scale
        ).astype(bf16)
        out_ref[:, 2 * width + start : 2 * width + start + HDIM] = left_product(
            probs.astype(bf16), d_out, bf16
        )


def attend(kernel, operands, documents, columns, name):
    seq_len, width = operands[0].shape
    docs_row = jnp.broadcast_to(documents[None, :], (8, seq_len))
    docs_col = jnp.broadcast_to(documents[:, None], (seq_len, LANES))
    return pl.pallas_call(
        kernel,
        out_shape=jax.ShapeDtypeStruct((seq_len, columns), bf16),
        compiler_params=pltpu.CompilerParams(vmem_limit_bytes=24 * MIB),
        cost_estimate=pl.CostEstimate(
            flops=10 * seq_len * seq_len * width,
            bytes_accessed=16 * seq_len * width,
            transcendentals=seq_len * seq_len * width // HDIM,
        ),
        name=name,
    )(*operands, docs_row, docs_col)


def core_swap(v):
    return lax.ppermute(v, "mp", [(0, 1), (1, 0), (2, 3), (3, 2)])


def chip_swap(v):
    return lax.ppermute(v, "mp", [(0, 2), (2, 0), (1, 3), (3, 1)])


def sum_mp(v):
    v = v + core_swap(v)
    return v + chip_swap(v)


def dp_permute(v, pairs):
    return lax.ppermute(v, "dp", pairs)


X_SWAP = [(i, i ^ 1) for i in range(8)]
Z_MID = [(2, 4), (4, 2), (3, 5), (5, 3)]
Z_NEAR = [(0, 2), (2, 0), (1, 3), (3, 1), (4, 6), (6, 4), (5, 7), (7, 5)]
Z_FAR = [(0, 4), (4, 0), (1, 5), (5, 1), (2, 6), (6, 2), (3, 7), (7, 3)]
TAIL = (192,)
PAIRS = {"x": X_SWAP, "near": Z_NEAR, "mid": Z_MID}


def sum_dp_small(v):
    if lax.axis_size("dp") != 8:
        return lax.psum(v, "dp")
    v = v + dp_permute(v, X_SWAP)
    v = v + dp_permute(v, Z_NEAR)
    return v + dp_permute(v, Z_FAR)


def widen(v):
    return v.astype(f32)


def add_low(left, right):
    return (widen(left) + widen(right)).astype(bf16)


def pack(grad):
    rows, columns = grad.shape
    groups = grad.reshape(rows, columns // LANES, LANES)
    return jnp.transpose(groups, (1, 0, 2)).reshape(rows * columns // LANES, LANES)


def grad_kernel(slabs, left_ref, right_ref, *refs):
    out_ref = refs[-1]
    rows = left_ref.shape[1]
    total = left_product(left_ref[...], right_ref[...])
    for j in range(slabs):
        out_ref[j * rows : (j + 1) * rows] = total[:, j * LANES : (j + 1) * LANES].astype(bf16)


def packed_grad(left_rows, right_rows, total_rows=None, at=0, into=None):
    tokens_here, rows = left_rows.shape
    groups = right_rows.shape[1] // LANES
    slabs = 4 if groups % 4 == 0 else 3
    if total_rows is None:
        total_rows = groups * rows
    specs = [
        pl.BlockSpec((tokens_here, rows), lambda i: (0, 0)),
        pl.BlockSpec((tokens_here, slabs * LANES), lambda i: (0, i)),
    ]
    operands = [left_rows, right_rows]
    aliases = {}
    if into is not None:
        specs.append(pl.BlockSpec(memory_space=pltpu.HBM))
        operands.append(into)
        aliases = {2: 0}
    first = at // (slabs * rows)
    return pl.pallas_call(
        lambda *refs: grad_kernel(slabs, *refs),
        grid=(groups // slabs,),
        in_specs=specs,
        out_specs=pl.BlockSpec((slabs * rows, LANES), lambda i: (first + i, 0)),
        out_shape=jax.ShapeDtypeStruct((total_rows, LANES), bf16),
        input_output_aliases=aliases,
        compiler_params=pltpu.CompilerParams(vmem_limit_bytes=20 * MIB),
        cost_estimate=pl.CostEstimate(
            flops=2 * tokens_here * rows * groups * LANES,
            bytes_accessed=4 * rows * groups * LANES,
            transcendentals=0,
        ),
        name="weight_grad",
    )(*operands)


def unpack(packed, rows):
    groups = packed.reshape(packed.shape[0] // rows, rows, LANES)
    return widen(jnp.transpose(groups, (1, 0, 2)).reshape(rows, -1))


SENDS = {
    "x": (("x1", 0, 2), ("zx", 2, 2), ("xf", 5, 2)),
    "in": (("xi", 1, 2), ("zi", 0, 4)),
    "mid": (("zm", 1, 2), ("xm", 2, 1), ("xn", 3, 1), ("zn", 3, 2)),
    "out": (("xo", 4, 2), ("zo", 4, 4)),
    "held": (("h", 1, 2), ("sz", 1, 2), ("sx", 2, 1)),
}


def layout(chunks):
    found = {}
    for channel, parts in SENDS.items():
        at, spots = 0, {}
        for name, stage, count in parts:
            if stage in chunks:
                spots[name] = (at, chunks[stage], count)
                at += chunks[stage] * count
        if at:
            found[channel] = (spots, at)
    into, out = found.pop("in", ({}, 0)), found.pop("out", ({}, 0))
    if into[1] or out[1]:
        found["near"] = ({**into[0], **out[0]}, max(into[1], out[1]), into[1] != out[1])
    return found


def chunk_rows(first, chunk, at, count):
    if isinstance(at, int):
        return pl.ds(first + at * chunk, count * chunk)
    return pl.ds(pl.multiple_of(first + at * chunk, 16), count * chunk)


def round_kernel(chunks, in_names, out_names, before, after, at0, at1, flags_ref, *refs):
    ins = dict(zip(in_names, refs[: len(in_names)]))
    refs = refs[len(in_names) :]
    outs = dict(zip(out_names, refs[: len(out_names)]))
    refs = refs[len(out_names) :]
    own_ref, sems = refs
    x, high, middle = flags_ref[0], flags_ref[1], flags_ref[2]
    low, outer = 1 - high, 1 - middle

    def part(spots, ref, name, at, count):
        first, chunk, whole = spots[0][name]
        return ref.at[chunk_rows(first, chunk, at, whole if count is None else count)]

    def came(channel, name, prefix, at=0, count=None):
        return part(before[channel], ins[prefix + channel], name, at, count)

    def goes(channel, name, at=0, count=None):
        return part(after[channel], outs[channel], name, at, count)

    def got(*spot):
        return came(*spot)[...]

    def put(channel, name, value):
        goes(channel, name)[...] = value

    def put_joined(channel, name, mine, other, second):
        half = after[channel][0][name][2] // 2
        goes(channel, name, second * half, half)[...] = mine
        goes(channel, name, (1 - second) * half, half)[...] = other

    copies = []

    def copy(source, target, when=None):
        move = pltpu.make_async_copy(source, target, sems.at[len(copies)])
        copies.append((move, when))
        if when is None:
            move.start()
        else:
            pl.when(when == 1)(move.start)
        return move

    def finish(move, when):
        if when is None:
            move.wait()
        else:
            pl.when(when == 1)(move.wait)

    if 1 in chunks:
        c = chunks[1]
        one = copy(ins["g1"].at[chunk_rows(at1, c, 2 * x, 2)], own_ref.at[chunk_rows(0, c, 0, 2)])
        two = copy(ins["g1"].at[chunk_rows(at1, c, 4, 4)], own_ref.at[chunk_rows(0, c, 2, 4)])
    if "near" in outs and after["near"][2]:
        outs["near"][...] = jnp.zeros_like(outs["near"])
    if 0 in chunks:
        c = chunks[0]
        copy(ins["g0"].at[chunk_rows(at0, c, 2 * (1 - x), 2)], goes("x", "x1"))
        copy(ins["g0"].at[chunk_rows(at0, c, 4, 4)], goes("near", "zi"), outer)
    if 5 in chunks:
        copy(came("near", "zo", "p_"), outs["fz"], middle)
        copy(came("near", "zo", "r_"), outs["fz"], outer)
    if 6 in chunks:
        c = chunks[6]
        copy(came("x", "xf", "p_"), outs["fx"].at[chunk_rows(0, c, 2 * x, 2)])
        copy(came("x", "xf", "r_"), outs["fx"].at[chunk_rows(0, c, 2 * (1 - x), 2)])
    if 2 in chunks:
        put("mid", "xm", add_low(got("held", "h", "p_", low, 1), got("near", "xi", "r_", low, 1)))
        put("held", "sx", add_low(got("held", "h", "p_", high, 1), got("near", "xi", "r_", high, 1)))
        put("x", "zx", add_low(got("held", "sz", "p_"), got("mid", "zm", "r_")))
    if 3 in chunks:
        put("mid", "xn", add_low(got("held", "sx", "p_"), got("mid", "xm", "r_")))
        put("mid", "zn", add_low(got("x", "zx", "p_"), got("x", "zx", "r_")))
    if 4 in chunks:

        @pl.when(middle == 1)
        def _():
            put_joined("near", "xo", got("mid", "xn", "p_"), got("mid", "xn", "r_"), high)
            put_joined("near", "zo", got("mid", "zn", "p_"), got("mid", "zn", "r_"), high)

    if 5 in chunks:

        @pl.when(middle == 1)
        def _():
            put("x", "xf", got("near", "xo", "p_"))

        @pl.when(middle == 0)
        def _():
            put("x", "xf", got("near", "xo", "r_"))

    if 1 in chunks:
        c = chunks[1]
        one.wait()
        two.wait()
        own = add_low(own_ref[chunk_rows(0, c, 0, 2)], got("x", "x1", "r_"))
        put("held", "h", own)

        @pl.when(middle == 0)
        def _():
            put("near", "xi", own)

        away, mine = 2 * low, 2 * high
        put(
            "mid",
            "zm",
            add_low(own_ref[chunk_rows(0, c, 2 + away, 2)], got("near", "zi", "r_", away, 2)),
        )
        put(
            "held",
            "sz",
            add_low(own_ref[chunk_rows(0, c, 2 + mine, 2)], got("near", "zi", "r_", mine, 2)),
        )
    for move, when in copies[2 if 1 in chunks else 0 :]:
        finish(move, when)


NEEDS = {
    0: (),
    1: ("r_x", "r_near"),
    2: ("p_held", "r_near", "r_mid"),
    3: ("p_held", "r_mid", "p_x", "r_x"),
    4: ("p_mid", "r_mid"),
    5: ("p_near", "r_near"),
    6: ("p_x", "r_x"),
}


class RowSums:
    def __init__(self):
        place = lax.axis_index("dp")
        x, z = place % 2, place // 2
        high = (z >= 2).astype(jnp.int32)
        middle = ((z == 1) | (z == 2)).astype(jnp.int32)
        self.flags = jnp.stack([x.astype(jnp.int32), high, middle])
        self.flying = {}
        self.values = {}
        self.spots = {}
        self.sizes = {}
        self.done = {}
        self.last = None
        self.whole = lax.axis_size("dp") == 8

    def round(self, key, source, chain):
        if not self.whole:
            if key is not None:
                array, first, size = source
                total = lax.psum(array[first : first + 8 * size], "dp")
                self.done[key] = [total[: 4 * size], total[4 * size :]]
            return chain
        moved = {stage + 1: name for stage, name in self.flying.items()}
        if key is not None:
            moved[0] = key
            self.sizes[key] = source[2]
        self.flying = {stage: name for stage, name in moved.items() if stage < 6}
        stages = {stage: self.sizes[name] for stage, name in sorted(moved.items())}
        before, after = self.spots, layout(stages)
        wanted = sorted({name for stage in stages for name in NEEDS[stage]})
        in_hbm = pl.BlockSpec(memory_space=pltpu.HBM)
        in_vmem = pl.BlockSpec(memory_space=pltpu.VMEM)
        operands, specs, in_names = [], [], []
        at0 = at1 = 0
        if 0 in moved:
            in_names.append("g0")
            operands.append(source[0])
            specs.append(in_hbm)
            at0 = source[1]
        if 1 in moved:
            in_names.append("g1")
            operands.append(self.last[0])
            specs.append(in_hbm)
            at1 = self.last[1]
        for name in wanted:
            in_names.append(name)
            operands.append(self.values[name])
            specs.append(in_vmem)
        out_names = list(after)
        counts = [after[name][1] for name in out_names]
        out_specs = [in_vmem] * len(counts)
        for stage, name in ((5, "fz"), (6, "fx")):
            if stage in moved:
                out_names.append(name)
                counts.append(4 * stages[stage])
                out_specs.append(in_hbm)
        touched = 80 * LANES * max(stages.values())

        def body(*refs):
            round_kernel(stages, in_names, out_names, before, after, at0, at1, *refs)

        results = pl.pallas_call(
            body,
            in_specs=[pl.BlockSpec(memory_space=pltpu.SMEM)] + specs,
            out_specs=out_specs,
            out_shape=[jax.ShapeDtypeStruct((count, LANES), bf16) for count in counts],
            scratch_shapes=[
                pltpu.VMEM((6 * stages.get(1, 16), LANES), bf16),
                pltpu.SemaphoreType.DMA((8,)),
            ],
            compiler_params=pltpu.CompilerParams(vmem_limit_bytes=6 * MIB),
            cost_estimate=pl.CostEstimate(
                flops=touched, bytes_accessed=touched, transcendentals=0
            ),
            name="round",
        )(self.flags, *operands)
        results = dict(zip(out_names, results))
        if 5 in moved:
            self.done[moved[5]] = [results.pop("fz")]
        if 6 in moved:
            self.done[moved[6]].insert(0, results.pop("fx"))
        if 0 in moved:
            self.last = source
        self.spots = after
        if chain is not None:
            chain = lax.optimization_barrier((results, chain))[1]
        self.values = {"p_" + name: value for name, value in results.items()}
        for channel, pairs in PAIRS.items():
            if channel in results:
                self.values["r_" + channel] = dp_permute(results[channel], pairs)
        return chain


def buckets(name, packed, sizes):
    found, at = [], 0
    while at < packed.shape[0]:
        size = sizes[min(len(found), len(sizes) - 1)]
        found.append(((name, len(found)), (packed, at, size)))
        at += 8 * size
    assert at == packed.shape[0]
    return found


def unpack_kernel(starts, *refs):
    out_ref = refs[-1]
    step = pl.program_id(0)
    for number, ref in enumerate(refs[:-1]):

        @pl.when((starts[number] <= step) & (step < starts[number + 1]))
        def _(ref=ref):
            out_ref[...] = widen(ref[...])


def unpack_parts(parts, rows, start=0, length=None):
    if length is not None:
        at, kept = 0, []
        for part in parts:
            if start <= at < start + length:
                kept.append(part)
            at += part.shape[0]
        parts = kept
    piece = math.gcd(rows, *[part.shape[0] for part in parts])
    starts = [0]
    for part in parts:
        starts.append(starts[-1] + part.shape[0] // piece)
    steps, per_group = starts[-1], rows // piece
    columns = steps // per_group * LANES

    def spec(first, last):
        return pl.BlockSpec((piece, LANES), lambda i: (jnp.clip(i - first, 0, last - first - 1), 0))

    return pl.pallas_call(
        lambda *refs: unpack_kernel(starts, *refs),
        grid=(steps,),
        in_specs=[spec(starts[n], starts[n + 1]) for n in range(len(parts))],
        out_specs=pl.BlockSpec((piece, LANES), lambda i: (i % per_group, i // per_group)),
        out_shape=jax.ShapeDtypeStruct((rows, columns), f32),
        compiler_params=pltpu.CompilerParams(vmem_limit_bytes=12 * MIB),
        cost_estimate=pl.CostEstimate(
            flops=rows * columns, bytes_accessed=6 * rows * columns, transcendentals=0
        ),
        name="unpack",
    )(*parts)


def per_device(
    tokens,
    cotangent,
    doc_starts,
    valid_len,
    gain_mixer,
    mixer_in_x,
    mixer_in_z,
    conv_weight,
    conv_bias,
    mixer_proj,
    delta_proj,
    delta_bias,
    decay_log,
    skip_weight,
    mixer_out,
    gain_first,
    gate_first,
    up_first,
    down_first,
    gain_attn,
    query_weight,
    key_weight,
    value_weight,
    output_weight,
    gain_second,
    gate_second,
    up_second,
    down_second,
):
    local_rows, width = tokens.shape
    seq_len = local_rows * 4
    place = lax.axis_index("mp")
    chip, core = place // 2, place % 2
    documents = document_ids(doc_starts[0], valid_len[0], seq_len)
    before = jnp.concatenate([jnp.full((1,), -1, jnp.int32), documents[:-1]])
    carry_on = (before == documents).astype(f32)
    places = jnp.arange(seq_len, dtype=jnp.int32)
    def both_halves(mine):
        other = chip_swap(mine)
        return jnp.stack([jnp.where(chip == 0, mine, other), jnp.where(chip == 0, other, mine)])

    def spread(mine):
        other = core_swap(mine)
        joined = jnp.stack(
            [jnp.where(core == 0, mine, other), jnp.where(core == 0, other, mine)], axis=1
        )
        return joined.reshape(seq_len, width)

    def half_rows(rows, which):
        cut = rows.reshape(2, 2, local_rows, rows.shape[1])
        return lax.dynamic_index_in_dim(cut, which, 1, keepdims=False).reshape(
            2 * local_rows, rows.shape[1]
        )

    def collect(pairs, multiply):
        away = multiply(half_rows(pairs[0][0], 1 - core), pairs[0][1])
        mine = multiply(half_rows(pairs[0][0], core), pairs[0][1])
        for rows, weight in pairs[1:]:
            away = away + multiply(half_rows(rows, 1 - core), weight)
            mine = mine + multiply(half_rows(rows, core), weight)
        mine = mine + widen(core_swap(away.astype(bf16)))
        mine = mine + widen(chip_swap(mine.astype(bf16)))
        return mine.reshape(2, local_rows, width)

    def ffn_forward(stream, gain_vec, gate_w, up_w, down_w):
        gathered = spread(rms_apply(stream, gain_vec).astype(bf16))
        gate_act = product(gathered, gate_w)
        up_act = product(gathered, up_w)
        hidden = (jax.nn.silu(gate_act) * up_act).astype(bf16)
        return (
            stream + collect(((hidden, down_w),), product),
            (stream, gathered, gate_act, up_act, hidden),
        )

    def ffn_pointwise(d_hidden, kept_state):
        _, _, gate_act, up_act, _ = kept_state
        sigmoid_gate = jax.nn.sigmoid(gate_act)
        d_gate = (
            d_hidden * up_act * sigmoid_gate * (1.0 + gate_act * (1.0 - sigmoid_gate))
        ).astype(bf16)
        return d_gate, (d_hidden * gate_act * sigmoid_gate).astype(bf16)

    def norm_backward(stream_grad, stream, gain_vec, d_normed):
        d_stream, d_gain = jax.vjp(rms_apply, stream, gain_vec)[1](d_normed)
        return stream_grad + d_stream, d_gain

    streams = [RowSums(), RowSums()]
    chunk = width // 4
    queue = []
    turn = [0]
    wanted = {}
    found = {}
    fresh = []

    def push(name, packed, rows, sizes=(chunk,)):
        parts = buckets(name, packed, sizes)
        wanted[name] = (rows, [key for key, _ in parts])
        queue.extend(parts)

    def unpack_finished(limit):
        done = {}
        for stream in streams:
            done.update(stream.done)
        for name, (rows, keys) in list(wanted.items()):
            if limit and all(len(done.get(key, ())) == 2 for key in keys):
                limit -= 1
                parts = [part for key in keys for part in done[key]]
                del wanted[name]
                if rows:
                    found[name] = unpack_parts(parts, rows)
                    fresh.append(name)
                else:
                    pieces = heads_width * width // LANES
                    for n, head_name in enumerate(("query", "key", "value")):
                        found[head_name] = unpack_parts(parts, width, n * pieces, pieces)
                        fresh.append(head_name)
                    found["output"] = unpack_parts(parts, heads_width, 3 * pieces, pieces)
                    fresh.append("output")

    def tick(chain=()):
        stream = streams[turn[0] % 2]
        turn[0] += 1
        if not queue and not stream.flying:
            return chain
        key, source = queue.pop(0) if queue else (None, None)
        names = list(fresh)
        fresh.clear()
        ready, chain = stream.round(key, source, ([found[name] for name in names], chain))
        found.update(zip(names, ready))
        unpack_finished(1)
        return chain

    def collect_back(grads, weights):
        if isinstance(grads, tuple):
            away = [half_rows(rows, 1 - core) for rows in grads]
            mine = [half_rows(rows, core) for rows in grads]
        else:
            cut = grads.shape[1] // len(weights)
            away, mine = half_rows(grads, 1 - core), half_rows(grads, core)
            away = [away[:, n * cut : (n + 1) * cut] for n in range(len(weights))]
            mine = [mine[:, n * cut : (n + 1) * cut] for n in range(len(weights))]
        away = sum(right_product(rows, weight) for rows, weight in zip(away, weights))
        mine = sum(right_product(rows, weight) for rows, weight in zip(mine, weights))
        away, mine = tick((away.astype(bf16), mine))
        mine = mine + widen(core_swap(away))
        low, mine = tick((mine.astype(bf16), mine))
        arrived = chip_swap(low)
        mine = tick(mine) + widen(arrived)
        return tick(mine).reshape(2, local_rows, width)

    stream_zero = widen(both_halves(tokens))
    cotangent_rows = both_halves(cotangent)
    gathered_mixer = spread(rms_apply(stream_zero, gain_mixer).astype(bf16))
    mixer_x = product(gathered_mixer, mixer_in_x)
    gate_values = product(gathered_mixer, mixer_in_z)

    def conv_part(values, weight, bias_vec):
        return causal_conv(values, weight, bias_vec, documents)

    activated, conv_back = jax.vjp(conv_part, mixer_x, conv_weight, conv_bias)
    act_low = activated.astype(bf16)
    mixer_feats = sum_mp(product(act_low, mixer_proj))
    delta_low = mixer_feats[:, :RANK].astype(bf16)
    delta_pre = product(delta_low, delta_proj) + delta_bias[None, :]
    state_shape = (seq_len, STATE, LANES)
    in_wide = jnp.broadcast_to(mixer_feats[:, RANK : RANK + STATE, None], state_shape)
    out_wide = jnp.broadcast_to(mixer_feats[:, RANK + STATE :, None], state_shape)
    keep_wide = jnp.broadcast_to(carry_on[:, None], (seq_len, LANES))
    decay_rates = -jnp.exp(decay_log.T)
    skip_row = skip_weight[None, :]
    scanned_low, result, states = scan_fwd(
        activated, delta_pre, gate_values, keep_wide, in_wide, out_wide, decay_rates, skip_row
    )
    stream_one = stream_zero + collect(((scanned_low, mixer_out),), product)
    stream_two, kept_first = ffn_forward(stream_one, gain_first, gate_first, up_first, down_first)
    gathered_attn = spread(rms_apply(stream_two, gain_attn).astype(bf16))
    queries = product(gathered_attn, query_weight, bf16)
    key_rows = product(gathered_attn, key_weight, bf16)
    value_rows = product(gathered_attn, value_weight, bf16)
    heads_width = queries.shape[1]
    attended_flat = attend(
        attend_forward_kernel,
        (queries, key_rows, value_rows),
        documents,
        heads_width,
        "attend_forward",
    )
    stream_three = stream_two + collect(((attended_flat, output_weight),), product)
    stream_four, kept_second = ffn_forward(
        stream_three, gain_second, gate_second, up_second, down_second
    )
    mixed_out = lax.dynamic_index_in_dim(stream_four, chip, 0, keepdims=False).astype(bf16)

    own_places = (
        jnp.arange(2, dtype=jnp.int32)[:, None] * (2 * local_rows)
        + core * local_rows
        + jnp.arange(local_rows, dtype=jnp.int32)[None, :]
    )
    live_rows = (own_places < valid_len[0]).astype(f32)
    stream_grad = widen(cotangent_rows) * live_rows[..., None]
    d_branch = spread(stream_grad.astype(bf16))
    push("down_second", packed_grad(kept_second[4], d_branch), down_second.shape[0])
    d_branch = tick(d_branch)
    d_gate, d_up = ffn_pointwise(right_product(d_branch, down_second), kept_second)
    push("gate_second", packed_grad(kept_second[1], d_gate), width)
    push("up_second", packed_grad(kept_second[1], d_up), width)
    d_gate, d_up = tick((d_gate, d_up))
    d_normed = collect_back((d_gate, d_up), (gate_second, up_second))
    stream_grad, d_gain_second = norm_backward(stream_grad, kept_second[0], gain_second, d_normed)
    d_branch = spread(stream_grad.astype(bf16))
    d_attended = right_product(d_branch, output_weight, bf16)
    d_attended = tick(d_attended)
    d_heads = attend(
        attend_backward_kernel,
        (queries, key_rows, value_rows, d_attended),
        documents,
        3 * heads_width,
        "attend_backward",
    )
    heads_rows = width * 3 * heads_width // LANES
    attn_rows = heads_rows + attended_flat.shape[1] * width // LANES
    attn_packed = packed_grad(
        attended_flat,
        d_branch,
        attn_rows,
        heads_rows,
        packed_grad(gathered_attn, d_heads, attn_rows),
    )
    push("attn", attn_packed, 0)
    d_heads = tick(d_heads)
    d_normed = collect_back(d_heads, (query_weight, key_weight, value_weight))
    stream_grad, d_gain_attn = norm_backward(stream_grad, stream_two, gain_attn, d_normed)
    d_branch = spread(stream_grad.astype(bf16))
    d_gate, d_up = ffn_pointwise(right_product(d_branch, down_first), kept_first)
    push("down_first", packed_grad(kept_first[4], d_branch), down_first.shape[0])
    push("gate_first", packed_grad(kept_first[1], d_gate), width)
    push("up_first", packed_grad(kept_first[1], d_up), width)
    d_gate, d_up = tick((d_gate, d_up))
    d_normed = collect_back((d_gate, d_up), (gate_first, up_first))
    stream_grad, d_gain_first = norm_backward(stream_grad, kept_first[0], gain_first, d_normed)
    d_branch = spread(stream_grad.astype(bf16))
    d_scanned = right_product(d_branch, mixer_out)
    channels = mixer_proj.shape[0]
    push("mixer_out", packed_grad(scanned_low, d_branch), channels)
    d_scanned = tick(d_scanned)
    d_scanned = tick(d_scanned)
    scan_inputs = (
        activated, delta_pre, gate_values, result, d_scanned,
        keep_wide, in_wide, out_wide, decay_rates, skip_row, states,
    )
    later = list(scan_bwd(*scan_inputs))
    later[-1] = tick(later[-1])
    (d_act_scan, d_delta_low, d_gate_low, d_in_map, d_out_map, d_rates, grad_skip, d_bias, _) = (
        scan_bwd(*scan_inputs, before=later)
    )
    push("in_z", packed_grad(gathered_mixer, d_gate_low), width)
    d_delta_low = tick(d_delta_low)
    d_feats = sum_mp(
        jnp.concatenate(
            [
                right_product(d_delta_low, delta_proj),
                d_in_map,
                d_out_map,
            ],
            axis=1,
        ).astype(bf16)
    )
    d_feats = tick(d_feats)
    d_activated = d_act_scan + right_product(d_feats, mixer_proj)
    d_mixer_x, grad_conv_weight, grad_conv_bias = conv_back(d_activated)
    d_mixer_x = d_mixer_x.astype(bf16)
    push("in_x", packed_grad(gathered_mixer, d_mixer_x), width, TAIL)
    d_mixer_x = tick(d_mixer_x)
    d_normed = collect_back((d_mixer_x, d_gate_low), (mixer_in_x, mixer_in_z))
    stream_grad, d_gain_mixer = norm_backward(stream_grad, stream_zero, gain_mixer, d_normed)
    input_grad = lax.dynamic_index_in_dim(stream_grad, chip, 0, keepdims=False)
    input_grad = tick(input_grad)
    joint = jnp.concatenate(
        [left_product(act_low, d_feats, bf16), pack(left_product(delta_low, d_delta_low, bf16))]
    )
    joint = widen(sum_dp_small(tick(joint)))
    little = jnp.concatenate(
        [grad_conv_weight, grad_conv_bias[None], d_bias, d_rates * decay_rates, grad_skip]
    )
    little = sum_dp_small(tick(little))
    gain_grads = 0.5 * sum_mp(jnp.stack([d_gain_mixer, d_gain_first, d_gain_attn, d_gain_second]))
    gain_grads = sum_dp_small(tick(gain_grads))
    grad_mixer_proj = joint[:channels]
    grad_delta_proj = unpack(joint[channels:], RANK)

    while queue or any(stream.flying for stream in streams):
        tick()
    unpack_finished(len(wanted))

    return (
        mixed_out,
        input_grad,
        gain_grads[0],
        found["in_x"],
        found["in_z"],
        little[:CONV],
        little[CONV],
        grad_mixer_proj,
        grad_delta_proj,
        little[CONV + 1],
        little[CONV + 2 : CONV + 2 + STATE].T,
        little[CONV + 2 + STATE],
        found["mixer_out"],
        gain_grads[1],
        found["gate_first"],
        found["up_first"],
        found["down_first"],
        gain_grads[2],
        found["query"],
        found["key"],
        found["value"],
        found["output"],
        gain_grads[3],
        found["gate_second"],
        found["up_second"],
        found["down_second"],
    )


def solution(mesh):
    placed = (
        P(("dp", "mp"), None),
        P(("dp", "mp"), None),
        P("dp", None),
        P("dp"),
        P(),
        P(None, "mp"),
        P(None, "mp"),
        P(None, "mp"),
        P("mp"),
        P("mp", None),
        P(None, "mp"),
        P("mp"),
        P("mp", None),
        P("mp"),
        P("mp", None),
        P(),
        P(None, "mp"),
        P(None, "mp"),
        P("mp", None),
        P(),
        P(None, "mp"),
        P(None, "mp"),
        P(None, "mp"),
        P("mp", None),
        P(),
        P(None, "mp"),
        P(None, "mp"),
        P("mp", None),
    )
    return jax.shard_map(
        per_device,
        mesh=mesh,
        in_specs=placed,
        out_specs=(
            P(("dp", "mp"), None),
            P(("dp", "mp"), None),
            P(),
            P(None, "mp"),
            P(None, "mp"),
            P(None, "mp"),
            P("mp"),
            P("mp", None),
            P(None, "mp"),
            P("mp"),
            P("mp", None),
            P("mp"),
            P("mp", None),
            P(),
            P(None, "mp"),
            P(None, "mp"),
            P("mp", None),
            P(),
            P(None, "mp"),
            P(None, "mp"),
            P(None, "mp"),
            P("mp", None),
            P(),
            P(None, "mp"),
            P(None, "mp"),
            P("mp", None),
        ),
        check_vma=False,
    )
```
